512 devices in a mesh: head: 8 (over z_lo), outer: 8 (over y, z_hi), inner: 8 (over x, core).
Axes of the slice: x: 4, y: 4, z: 16 (z_hi: 2, z_lo: 8; z = z_hi * 8 + z_lo), core: 2. Of those that a mesh axis runs over, the one named last changes fastest.
Arguments:
- query_states: bfloat16 [8, 4096, 4096], P('head', ('outer', 'inner')), may hold values from -24 to 24
- key_states: bfloat16 [8, 4096, 4096], P('head', ('outer', 'inner')), may hold values from -24 to 24
- value_states: bfloat16 [8, 4096, 4096], P('head', ('outer', 'inner')), may hold values from -6 to 6
- output_grad: bfloat16 [8, 4096, 4096], P('head', ('outer', 'inner')), may hold values from -1.5 to 1.5
- saved_offset: float32 [8, 4096, 32], P(None, ('outer', 'inner'), 'head'), may hold values from -6 to 6
- rest_mass: float32 [8, 4096, 32], P(None, ('outer', 'inner'), 'head'), may hold values from 0 to 16
Outputs:
- query_grad: bfloat16 [8, 4096, 4096], P(None, ('outer', 'inner'), 'head')
- key_grad: float32 [8, 4096, 4096], P(None, ('outer', 'inner'), 'head')
- value_grad: float32 [8, 4096, 4096], P(None, ('outer', 'inner'), 'head')
The draws below stay inside these ranges and needn't reach their ends.
All inputs are finite; a program needn't handle non-finite values.
Results may differ from the reference program's by a relative error of at most 0.012.
Values may be sent and summed in bfloat16 or wider, within the bound.
A program may use at most 128 MiB of HBM per device.

```python
import math
import jax
import jax.numpy as jnp
from jax import lax

HEADS = 32
HD = 128
TOK_DEV = 64
FEAT = 4096
TOKS_GROUP = 4096
N_HEAD = 8
N_OUTER = 8
N_INNER = 8


def drawn_keys(key):
    full_shape = (N_HEAD, TOKS_GROUP, HEADS, HD)
    normal_key = jax.random.fold_in(key, 0)
    scale_key = jax.random.fold_in(key, 2)
    normal_part = jnp.clip(jax.random.normal(normal_key, full_shape, jnp.float32), -4.0, 4.0)
    mixed = normal_part
    row_scale = jnp.exp(jax.random.uniform(scale_key, (N_HEAD, TOKS_GROUP, HEADS, 1), jnp.float32, minval=math.log(0.6), maxval=math.log(6.0)))
    states = mixed * row_scale
    return states


def draw_key_states(key, part):
    states = drawn_keys(key)
    return jnp.clip(states, -24.0, 24.0).reshape(N_HEAD, TOKS_GROUP, HEADS * HD).astype(jnp.bfloat16)


def draw_query_states(key, part):
    key = jax.random.fold_in(key, 11)
    full_shape = (N_HEAD, TOKS_GROUP, HEADS, HD)
    normal_key = jax.random.fold_in(key, 0)
    scale_key = jax.random.fold_in(key, 2)
    normal_part = jnp.clip(jax.random.normal(normal_key, full_shape, jnp.float32), -4.0, 4.0)
    row_scale = jnp.exp(jax.random.uniform(scale_key, (N_HEAD, TOKS_GROUP, HEADS, 1), jnp.float32, minval=math.log(0.5), maxval=math.log(2.0)))
    mixed = normal_part * row_scale
    return jnp.clip(mixed, -24.0, 24.0).reshape(N_HEAD, TOKS_GROUP, HEADS * HD).astype(jnp.bfloat16)


def level_of(stream_key, extent, cuts, low, high):
    def one(dim, shards_of):
        steps = jax.random.uniform(jax.random.fold_in(jax.random.fold_in(stream_key, 6), dim), (shards_of,), jnp.float32, low / len(cuts), high / len(cuts))
        return jnp.repeat(jnp.exp(steps), extent[dim] // shards_of).reshape((-1,) + (1,) * (len(extent) - dim - 1))

    level = one(*cuts[0])
    for cut in cuts[1:]:
        level = level * one(*cut)
    return level


def bell_draw(own_key, shape, spread, limit, cuts=(), kind=jnp.bfloat16):
    drawn = jax.random.normal(own_key, shape, jnp.float32) * spread
    if len(cuts) > 0:
        drawn = level_of(own_key, shape, cuts, -0.22, 0.18) * drawn
    return jnp.clip(drawn, min=-limit, max=limit).astype(kind)


def setup_inputs(seed: int = 0) -> dict:
    key_of = jax.random.split(jax.random.key(seed), 7)
    query_states = draw_query_states(jax.random.fold_in(key_of[6], 71), 0)
    key_states = draw_key_states(jax.random.fold_in(key_of[6], 71), 0)
    value_states = bell_draw(key_of[2], (N_HEAD, TOKS_GROUP, FEAT), 1.0, 6.0, ((0, 8), (1, 64)))
    output_grad = bell_draw(key_of[3], (N_HEAD, TOKS_GROUP, FEAT), 0.25, 1.5, ((0, 8), (1, 64)))
    saved_offset = bell_draw(key_of[4], (N_HEAD, TOKS_GROUP, HEADS), 1.5, 6.0, ((1, 64), (2, 8)), jnp.float32)
    rest_mass = jnp.clip(16.0 * jax.random.uniform(key_of[5], (N_HEAD, TOKS_GROUP, HEADS), jnp.float32) ** level_of(key_of[5], (N_HEAD, TOKS_GROUP, HEADS), ((1, 64), (2, 8)), -0.2, 0.2), 0.0, 16.0)
    return dict(query_states=query_states, key_states=key_states, value_states=value_states, output_grad=output_grad, saved_offset=saved_offset, rest_mass=rest_mass)


def to_blocks(array, cycle_size):
    leading, tokens, channels = array.shape
    per_block = tokens // cycle_size
    return array.reshape(leading, cycle_size, per_block, channels).transpose(1, 0, 2, 3).reshape(cycle_size, leading * per_block, channels)


def from_blocks(array, leading):
    cycle_size, tokens, channels = array.shape
    per_block = tokens // leading
    return array.reshape(cycle_size, leading, per_block, channels).transpose(1, 0, 2, 3).reshape(leading, cycle_size * per_block, channels)


def reference(query_states, key_states, value_states, output_grad, saved_offset, rest_mass):
    cycle_size = N_OUTER * N_INNER
    window = N_INNER // 2
    block_rows = N_HEAD * TOK_DEV
    score_scale = HD ** -0.5
    query_blocks = to_blocks(query_states, cycle_size).reshape(cycle_size, block_rows, HEADS, HD)
    key_blocks = to_blocks(key_states, cycle_size).reshape(cycle_size, block_rows, HEADS, HD)
    value_blocks = to_blocks(value_states, cycle_size).reshape(cycle_size, block_rows, HEADS, HD)
    grad_blocks = to_blocks(output_grad, cycle_size).reshape(cycle_size, block_rows, HEADS, HD)
    offset_blocks = to_blocks(saved_offset, cycle_size)
    rest_blocks = to_blocks(rest_mass, cycle_size)
    hop_offsets = jnp.arange(window, dtype=jnp.int32)

    def visit_block(carry, block_index):
        key_acc, value_acc = carry
        window_ids = ((block_index - hop_offsets) % cycle_size).astype(jnp.int32)
        query_rows = query_blocks[block_index].astype(jnp.float32)
        grad_rows = grad_blocks[block_index].astype(jnp.float32)
        window_keys = key_blocks[window_ids].reshape(window * block_rows, HEADS, HD).astype(jnp.float32)
        window_values = value_blocks[window_ids].reshape(window * block_rows, HEADS, HD).astype(jnp.float32)
        scores = jnp.einsum("qhd,khd->hqk", query_rows, window_keys) * score_scale
        row_max = jnp.max(scores, axis=-1)
        row_sum = jnp.sum(jnp.exp(scores - row_max[:, :, None]), axis=-1)
        rest_local = rest_blocks[block_index].T
        ceiling = jnp.maximum(row_max, rest_local)
        log_norm = ceiling + jnp.log(row_sum * jnp.exp(row_max - ceiling) + jnp.exp(rest_local - ceiling))
        weights = jnp.exp(scores - log_norm[:, :, None])
        weights_low = lax.optimization_barrier(weights.astype(jnp.bfloat16)).astype(jnp.float32)
        offset = offset_blocks[block_index].T
        dweights = jnp.einsum("qhd,khd->hqk", grad_rows, window_values)
        dscores = lax.optimization_barrier((weights * (dweights - offset[:, :, None])).astype(jnp.bfloat16)).astype(jnp.float32)
        query_term = jnp.einsum("hqk,khd->qhd", dscores, window_keys) * score_scale
        key_term = jnp.einsum("hqk,qhd->khd", dscores, query_rows) * score_scale
        value_term = jnp.einsum("hqk,qhd->khd", weights_low, grad_rows)
        key_acc = key_acc.at[window_ids].add(key_term.reshape(window, block_rows, HEADS * HD))
        value_acc = value_acc.at[window_ids].add(value_term.reshape(window, block_rows, HEADS * HD))
        return (key_acc, value_acc), query_term.reshape(block_rows, HEADS * HD).astype(jnp.bfloat16)

    empty = jnp.zeros((cycle_size, block_rows, HEADS * HD), jnp.float32)
    (key_acc, value_acc), query_out = lax.scan(visit_block, (empty, empty), jnp.arange(cycle_size, dtype=jnp.int32))
    key_out = jnp.roll(key_acc, window, axis=0)
    value_out = jnp.roll(value_acc, window, axis=0)
    return (from_blocks(query_out, N_HEAD), from_blocks(key_out, N_HEAD), from_blocks(value_out, N_HEAD))
```

```python
import functools
import math

import jax
import jax.numpy as jnp
from jax import lax
from jax.experimental import pallas as pl
from jax.experimental.pallas import tpu as pltpu
from jax.sharding import PartitionSpec as P

MESH = pl.DeviceIdType.MESH
F32 = jnp.float32
BF16 = jnp.bfloat16

KEY, VALUE, QUERY, GRAD = range(4)
WINDOW = 4
PEER_ORDER = (4, 3, 5, 2, 6, 1, 7)
BORDER_SLOT = {7: 1, 6: 2, 5: 3, 4: 4}
BORDER_SENDER = {7: 7, 6: 0, 5: 3, 4: 4}
LEAD = 1


def nt(a, b):
    return lax.dot_general(a, b, (((1,), (1,)), ((), ())), preferred_element_type=F32)


def nn(a, b):
    return lax.dot_general(a, b, (((1,), (0,)), ((), ())), preferred_element_type=F32)


def tn(a, b):
    return lax.dot_general(a, b, (((0,), (0,)), ((), ())), preferred_element_type=F32)


def kernel(
    keys, values, queries, grads, stats_in, query_out, key_out, value_out,
    blk, hop, aux, weights, dscores, key_acc, value_acc, row_factor,
    home_send, home_recv, own_sem, ring_send, ring_recv, hop_send, hop_recv,
    border_send, aux_send, aux_recv,
):
    h, o, i = lax.axis_index("head"), lax.axis_index("outer"), lax.axis_index("inner")
    arrays = (keys, values, queries, grads)
    heads = 4
    rows, size = 64, 128
    block = 8 * rows
    scale = float(size) ** -0.5
    scale2 = scale * math.log2(math.e)
    next_o, last_o = lax.rem(o + 1, 8), lax.rem(o + 7, 8)
    my_rows = pl.ds(pl.multiple_of(h * rows, rows), rows)

    def ahead(by):
        at = i + by
        return (h, jnp.where(at > 7, next_o, o), lax.rem(at, 8))

    def behind(by):
        at = i + 8 - by
        return (h, jnp.where(at < 8, last_o, o), lax.rem(at, 8))

    barrier = pltpu.get_barrier_semaphore()

    def greet(device):
        pl.semaphore_signal(barrier, inc=1, device_id=device, device_id_type=MESH)

    for d in range(1, 8):
        greet((lax.rem(h + d, 8), o, i))
    for d in range(1, WINDOW + 1):
        greet(behind(d))

    @pl.when(i == 3)
    def _():
        greet((h, o, 5))

    @pl.when(i == 0)
    def _():
        greet((h, o, 6))
        for d in range(8):
            for sender in BORDER_SENDER.values():
                greet((lax.rem(h + d, 8), last_o, sender))

    sends_border = (i == 0) | (i == 3) | (i == 4) | (i == 7)
    sends_hop = (i == 5) | (i == 6)
    relays = (i == 0) | (i == 3)

    for a in range(4):
        for j in range(heads):
            pltpu.make_async_copy(
                arrays[a].at[0, :, pl.ds(pl.multiple_of(h * 512 + j * size, size), size)],
                blk.at[0, a, j, my_rows, :],
                own_sem,
            ).start()

    pl.semaphore_wait(
        barrier, 7 + WINDOW + jnp.where(sends_border, 8, 0) + jnp.where(sends_hop, 1, 0)
    )

    def columns(t, j):
        return pl.ds(pl.multiple_of(t * 512 + j * size, size), size)

    def hop_copy(j, a, t):
        return pltpu.make_async_remote_copy(
            src_ref=arrays[a].at[0, :, columns(t, j)],
            dst_ref=hop.at[a, j, t],
            send_sem=hop_send,
            recv_sem=hop_recv.at[j, a],
            device_id=(h, o, jnp.where(i == 5, 3, 0)),
            device_id_type=MESH,
        )

    def border_copy(j, a, t, slot, source):
        return pltpu.make_async_remote_copy(
            src_ref=source,
            dst_ref=blk.at[slot, a, j, my_rows, :],
            send_sem=border_send,
            recv_sem=ring_recv.at[slot - 1, j, a],
            device_id=(t, next_o, 0),
            device_id_type=MESH,
        )

    def send_hops(j):
        for a in range(4):
            for t in range(8):
                hop_copy(j, a, t).start()

    def send_unit(j, a):
        for d in PEER_ORDER:
            t = lax.rem(h + d, 8)
            pltpu.make_async_remote_copy(
                src_ref=arrays[a].at[0, :, columns(t, j)],
                dst_ref=blk.at[0, a, j, my_rows, :],
                send_sem=home_send,
                recv_sem=home_recv.at[j, a],
                device_id=(t, o, i),
                device_id_type=MESH,
            ).start()

        @pl.when((i == 4) | (i == 7))
        def _():
            slot = jnp.where(i == 4, 4, 1)
            for d in range(8):
                t = lax.rem(h + d, 8)
                border_copy(j, a, t, slot, arrays[a].at[0, :, columns(t, j)]).start()

        @pl.when(relays)
        def _():
            slot = jnp.where(i == 0, 2, 3)
            pltpu.make_async_copy(hop.at[a, j], hop.at[a, j], hop_recv.at[j, a]).wait()
            for d in range(8):
                t = lax.rem(h + d, 8)
                border_copy(j, a, t, slot, hop.at[a, j, t]).start()

    def pass_on(slot, j, a):
        @pl.when(i < 7)
        def _():
            pltpu.make_async_remote_copy(
                src_ref=blk.at[slot, a, j],
                dst_ref=blk.at[slot + 1, a, j],
                send_sem=ring_send,
                recv_sem=ring_recv.at[slot, j, a],
                device_id=(h, o, lax.rem(i + 1, 8)),
                device_id_type=MESH,
            ).start()

    def aux_copy(j, by):
        return pltpu.make_async_remote_copy(
            src_ref=aux.at[0, j],
            dst_ref=aux.at[by, j],
            send_sem=aux_send,
            recv_sem=aux_recv.at[by - 1, j],
            device_id=ahead(by),
            device_id_type=MESH,
        )

    def norms(j):
        query = blk[0, QUERY, j]
        row_max = jnp.full((1, block), -jnp.inf, F32)
        for s in range(WINDOW):
            scores = nt(blk[s, KEY, j], query) * scale2
            weights[s] = scores
            row_max = jnp.maximum(row_max, jnp.max(scores, axis=0, keepdims=True))
        row_sum = jnp.zeros((1, block), F32)
        for s in range(WINDOW):
            e = jnp.exp2(weights[s] - row_max)
            weights[s] = e
            row_sum = row_sum + jnp.sum(e, axis=0, keepdims=True)
        rest = stats_in[j, 0:1, :] * math.log2(math.e)
        offset = stats_in[j, 1:2, :]
        ceiling = jnp.maximum(row_max, rest)
        total = row_sum * jnp.exp2(row_max - ceiling) + jnp.exp2(rest - ceiling)
        log_norm = ceiling + jnp.log2(total)
        row_factor[...] = jnp.exp2(row_max - log_norm)
        for r in range(4):
            lanes = slice(r * 128, (r + 1) * 128)
            aux[0, j, r : r + 1, :] = log_norm[:, lanes]
            aux[0, j, r + 4 : r + 5, :] = offset[:, lanes]
        for by in range(1, WINDOW + 1):
            aux_copy(j, by).start()

    def query_grads(j):
        grad = blk[0, GRAD, j]
        offset = stats_in[j, 1:2, :]
        factor = row_factor[...]
        acc = jnp.zeros((size, block), F32)
        for s in range(WINDOW):
            dweights = nt(blk[s, VALUE, j], grad)
            dscores[...] = ((weights[s] * factor) * (dweights - offset)).astype(BF16)
            acc = acc + tn(blk[s, KEY, j], dscores[...])
        query_out[:, pl.ds(pl.multiple_of(j * size, size), size)] = (acc.T * scale).astype(BF16)

    def key_grads(t, j):
        pltpu.make_async_copy(aux.at[t, j], aux.at[t, j], aux_recv.at[t - 1, j]).wait()
        log_norm = jnp.concatenate([aux[t, j, r : r + 1, :] for r in range(4)], axis=1)
        offset = jnp.concatenate([aux[t, j, r + 4 : r + 5, :] for r in range(4)], axis=1)
        query, grad = blk[t, QUERY, j], blk[t, GRAD, j]
        for part in range(4):
            at = pl.ds(part * 128, 128)
            scores = nt(blk[WINDOW, KEY, j, at, :], query) * scale2
            w = jnp.exp2(scores - log_norm)
            dweights = nt(blk[WINDOW, VALUE, j, at, :], grad)
            ds = (w * (dweights - offset)).astype(BF16)
            key_acc[at, :] += nn(ds, query)
            value_acc[at, :] += nn(w.astype(BF16), grad)

    def clear_accs():
        key_acc[...] = jnp.zeros_like(key_acc)
        value_acc[...] = jnp.zeros_like(value_acc)

    def write_key_grads(j):
        lanes = pl.ds(pl.multiple_of(j * size, size), size)
        key_out[:, lanes] = key_acc[...] * scale
        value_out[:, lanes] = value_acc[...]

    @pl.when(sends_hop)
    def _():
        def one(j, carry):
            send_hops(j)
            return carry

        lax.fori_loop(0, heads, one, 0)

    def first(j, carry):
        for a in range(4):
            send_unit(j, a)
        return carry

    lax.fori_loop(0, LEAD, first, 0)
    pltpu.make_async_copy(blk.at[0, 0, 0:2], blk.at[0, 0, 0:2], own_sem).wait()

    def ticks(jj, carry):
        for a in range(4):

            @pl.when(jj + LEAD < heads)
            def _():
                send_unit(jj + LEAD, a)

            @pl.when(jj < heads)
            def _():
                part = blk.at[0, a, jj, 0 : block - rows, :]
                pltpu.make_async_copy(part, part, home_recv.at[jj, a]).wait()
                pass_on(0, jj, a)

            for s in range(1, WINDOW + 1):
                b = (a - s) % 4
                j = jj if a >= s else jj - 1

                @pl.when((j >= 0) & (j < heads))
                def _():
                    part = blk.at[s, b, j]
                    pltpu.make_async_copy(part, part, ring_recv.at[s - 1, j, b]).wait()
                    if s < WINDOW:
                        pass_on(s, j, b)

            if a == 3:

                @pl.when(jj < heads)
                def _():
                    norms(jj)

            @pl.when(jj >= 1)
            def _():
                j = jj - 1
                if a == 0:
                    query_grads(j)
                elif a == 1:
                    clear_accs()
                    key_grads(1, j)
                    key_grads(2, j)
                elif a == 2:
                    key_grads(3, j)
                else:
                    key_grads(4, j)
                    write_key_grads(j)

        return carry

    lax.fori_loop(0, heads + 1, ticks, 0)

    part = blk.at[0, :, :, 0 : block - rows, :]
    pltpu.make_async_copy(part, part, home_send).wait()
    part = aux.at[1 : WINDOW + 1]
    pltpu.make_async_copy(part, part, aux_send).wait()

    @pl.when(i < 7)
    def _():
        part = blk.at[0:WINDOW]
        pltpu.make_async_copy(part, part, ring_send).wait()

    @pl.when(sends_border)
    def _():
        pltpu.make_async_copy(blk.at[0], blk.at[0], border_send).wait()

    @pl.when(sends_hop)
    def _():
        pltpu.make_async_copy(blk.at[0], blk.at[0], hop_send).wait()


def body(query_states, key_states, value_states, output_grad, saved_offset, rest_mass):
    stats = jnp.stack([rest_mass, saved_offset]).reshape(2, 512, 4).transpose(2, 0, 1)
    any_spec = pl.BlockSpec(memory_space=pl.ANY)
    vmem = pl.BlockSpec(memory_space=pltpu.VMEM)
    dma = pltpu.SemaphoreType.DMA
    outs = pl.pallas_call(
        kernel,
        out_shape=(
            jax.ShapeDtypeStruct((512, 512), BF16),
            jax.ShapeDtypeStruct((512, 512), F32),
            jax.ShapeDtypeStruct((512, 512), F32),
        ),
        in_specs=[any_spec] * 4 + [vmem],
        out_specs=(vmem,) * 3,
        scratch_shapes=[
            pltpu.VMEM((WINDOW + 1, 4, 4, 512, 128), BF16),
            pltpu.VMEM((4, 4, 8, 64, 128), BF16),
            pltpu.VMEM((WINDOW + 1, 4, 8, 128), F32),
            pltpu.VMEM((WINDOW, 512, 512), F32),
            pltpu.VMEM((512, 512), BF16),
            pltpu.VMEM((512, 128), F32),
            pltpu.VMEM((512, 128), F32),
            pltpu.VMEM((1, 512), F32),
            dma,
            dma((4, 4)),
            dma,
            dma,
            dma((WINDOW, 4, 4)),
            dma,
            dma((4, 4)),
            dma,
            dma,
            dma((WINDOW, 4)),
        ],
        compiler_params=pltpu.CompilerParams(
            collective_id=0, has_side_effects=True, vmem_limit_bytes=60 << 20
        ),
        cost_estimate=pl.CostEstimate(
            flops=7_500_000_000, bytes_accessed=5_000_000, transcendentals=8_400_000
        ),
    )(key_states, value_states, query_states, output_grad, stats)
    return tuple(out.reshape(8, 64, 512) for out in outs)


def solution(mesh):
    tokens = P("head", ("outer", "inner"), None)
    heads = P(None, ("outer", "inner"), "head")
    return jax.shard_map(
        body,
        mesh=mesh,
        in_specs=(tokens, tokens, tokens, tokens, heads, heads),
        out_specs=(heads, heads, heads),
        check_vma=False,
    )
```

```python
import functools
import math

import jax
import jax.numpy as jnp
from jax import lax
from jax.experimental import pallas as pl
from jax.experimental.pallas import tpu as pltpu
from jax.sharding import PartitionSpec as P

MESH = pl.DeviceIdType.MESH
F32 = jnp.float32
BF16 = jnp.bfloat16

KEY, QUERY, VALUE, GRAD = range(4)
UNITS = 16
WINDOW = 4
PEER_ORDER = (4, 3, 5, 2, 6, 1, 7)
BORDER_SENDERS = {0: (0, 4), 1: (7, 3)}
LEAD = 2
BORDER_LEAD = 3
HOP_LEAD = BORDER_LEAD + 2


def nt(a, b):
    return lax.dot_general(a, b, (((1,), (1,)), ((), ())), preferred_element_type=F32)


def nn(a, b):
    return lax.dot_general(a, b, (((1,), (0,)), ((), ())), preferred_element_type=F32)


def tn(a, b):
    return lax.dot_general(a, b, (((0,), (0,)), ((), ())), preferred_element_type=F32)


def kernel(
    keys, queries, values, grads, rest_in, offset_in, query_out, key_out, value_out,
    staged, blk, hop, aux, weights, dscores, key_acc, value_acc, row_factor, offsets,
    home_send, home_recv, own_sem, stage_sem, ring_send, ring_recv, hop_send, hop_recv,
    border_send, aux_send, aux_recv,
):
    h, o, i = lax.axis_index("head"), lax.axis_index("outer"), lax.axis_index("inner")
    inputs = (keys, queries, values, grads)
    heads = 4
    rows, size = 64, 128
    block = 8 * rows
    scale = float(size) ** -0.5
    scale2 = scale * math.log2(math.e)
    core = lax.rem(i, 2)
    sibling = i + 1 - 2 * core
    next_o, last_o = lax.rem(o + 1, 8), lax.rem(o + 7, 8)
    my_rows = pl.ds(pl.multiple_of(h * rows, rows), rows)

    def ahead(by):
        at = i + by
        return (h, jnp.where(at > 7, next_o, o), lax.rem(at, 8))

    def behind(by):
        at = i + 8 - by
        return (h, jnp.where(at < 8, last_o, o), lax.rem(at, 8))

    barrier = pltpu.get_barrier_semaphore()

    def greet(device):
        pl.semaphore_signal(barrier, inc=1, device_id=device, device_id_type=MESH)

    for receiver, senders in BORDER_SENDERS.items():

        @pl.when(i == receiver)
        def _():
            for d in range(8):
                for sender in senders:
                    greet((lax.rem(h + d, 8), last_o, sender))

    for d in range(1, 8):
        greet((lax.rem(h + d, 8), o, i))
    for d in range(1, WINDOW + 1):
        greet(behind(d))

    @pl.when(core == 0)
    def _():
        greet((h, o, sibling))

    @pl.when(i == 3)
    def _():
        greet((h, o, 5))

    @pl.when(i == 0)
    def _():
        greet((h, o, 6))

    sends_border = (i == 0) | (i == 3) | (i == 4) | (i == 7)
    sends_hop = (i == 5) | (i == 6)
    relays = (i == 0) | (i == 3)

    def stage(a):
        return pltpu.make_async_copy(inputs[a].at[0], staged.at[a], stage_sem.at[a])

    for a in range(4):
        stage(a).start()

    pl.semaphore_wait(
        barrier, 7 + WINDOW + core + jnp.where(sends_border, 8, 0) + jnp.where(sends_hop, 1, 0)
    )

    for a in range(4):
        stage(a).wait()

    for a in range(4):
        for j in range(heads):
            pltpu.make_async_copy(
                staged.at[a, :, pl.ds(pl.multiple_of(h * 512 + j * size, size), size)],
                blk.at[0, a, j, my_rows, :],
                own_sem,
            ).start()

    def columns(t, j):
        return pl.ds(pl.multiple_of(t * 512 + j * size, size), size)

    def hop_copy(j, a, t):
        return pltpu.make_async_remote_copy(
            src_ref=staged.at[a, :, columns(t, j)],
            dst_ref=hop.at[a, j, t],
            send_sem=hop_send,
            recv_sem=hop_recv.at[j, a],
            device_id=(h, o, jnp.where(i == 5, 3, 0)),
            device_id_type=MESH,
        )

    def border_copy(j, a, t, slot, source):
        return pltpu.make_async_remote_copy(
            src_ref=source,
            dst_ref=blk.at[slot, a, j, my_rows, :],
            send_sem=border_send,
            recv_sem=ring_recv.at[slot - 1, j, a],
            device_id=(t, next_o, jnp.where((i == 3) | (i == 7), 1, 0)),
            device_id_type=MESH,
        )

    def send_hops(j, a):
        @pl.when(sends_hop)
        def _():
            for t in range(8):
                hop_copy(j, a, t).start()

    def send_unit(j, a):
        for d in PEER_ORDER:
            t = lax.rem(h + d, 8)
            pltpu.make_async_remote_copy(
                src_ref=staged.at[a, :, columns(t, j)],
                dst_ref=blk.at[0, a, j, my_rows, :],
                send_sem=home_send,
                recv_sem=home_recv.at[j, a],
                device_id=(t, o, i),
                device_id_type=MESH,
            ).start()

    def send_border(j, a):
        @pl.when((i == 4) | (i == 7))
        def _():
            slot = jnp.where(i == 4, 4, 2)
            for d in range(8):
                t = lax.rem(h + d, 8)
                border_copy(j, a, t, slot, staged.at[a, :, columns(t, j)]).start()

        @pl.when(relays)
        def _():
            slot = jnp.where(i == 0, 2, 4)
            pltpu.make_async_copy(hop.at[a, j], hop.at[a, j], hop_recv.at[j, a]).wait()
            for d in range(8):
                t = lax.rem(h + d, 8)
                border_copy(j, a, t, slot, hop.at[a, j, t]).start()

    def pass_on(slot, to_slot, to, j, a):
        pltpu.make_async_remote_copy(
            src_ref=blk.at[slot, a, j],
            dst_ref=blk.at[to_slot, a, j],
            send_sem=ring_send,
            recv_sem=ring_recv.at[to_slot - 1, j, a],
            device_id=(h, o, to),
            device_id_type=MESH,
        ).start()

    def to_next_chip(slot, j, a):
        @pl.when(i < 6)
        def _():
            pass_on(slot, slot + 2, lax.rem(i + 2, 8), j, a)

    def to_sibling(slot, to_slot, from_core, j, a):
        @pl.when(core == from_core)
        def _():
            pass_on(slot, to_slot, sibling, j, a)

    def await_slot(s, j, a):
        part = blk.at[s, a, j]
        pltpu.make_async_copy(part, part, ring_recv.at[s - 1, j, a]).wait()

    def aux_copy(j, by):
        return pltpu.make_async_remote_copy(
            src_ref=aux.at[0, j],
            dst_ref=aux.at[by, j],
            send_sem=aux_send,
            recv_sem=aux_recv.at[by - 1, j],
            device_id=ahead(by),
            device_id_type=MESH,
        )

    def row_of(ref, j):
        return jnp.concatenate([ref[a, pl.ds(j, 1), :] for a in range(8)], axis=1)

    def norms(j):
        query = blk[0, QUERY, j]
        row_max = jnp.full((1, block), -jnp.inf, F32)
        for s in range(WINDOW):
            scores = nt(blk[s, KEY, j], query) * scale2
            weights[j, s] = scores
            row_max = jnp.maximum(row_max, jnp.max(scores, axis=0, keepdims=True))
        row_sum = jnp.zeros((1, block), F32)
        for s in range(WINDOW):
            e = jnp.exp2(weights[j, s] - row_max)
            weights[j, s] = e
            row_sum = row_sum + jnp.sum(e, axis=0, keepdims=True)
        rest = row_of(rest_in, j) * math.log2(math.e)
        offset = row_of(offset_in, j)
        offsets[j] = offset
        ceiling = jnp.maximum(row_max, rest)
        total = row_sum * jnp.exp2(row_max - ceiling) + jnp.exp2(rest - ceiling)
        log_norm = ceiling + jnp.log2(total)
        row_factor[j] = jnp.exp2(row_max - log_norm)
        for r in range(4):
            lanes = slice(r * 128, (r + 1) * 128)
            aux[0, j, r : r + 1, :] = log_norm[:, lanes]
            aux[0, j, r + 4 : r + 5, :] = offset[:, lanes]
        for by in range(1, WINDOW + 1):
            aux_copy(j, by).start()

    def query_grads(j):
        grad = blk[0, GRAD, j]
        offset = offsets[j]
        factor = row_factor[j]
        acc = jnp.zeros((size, block), F32)
        for s in range(WINDOW):
            dweights = nt(blk[s, VALUE, j], grad)
            dscores[...] = ((weights[j, s] * factor) * (dweights - offset)).astype(BF16)
            acc = acc + tn(blk[s, KEY, j], dscores[...])
        query_out[:, pl.ds(pl.multiple_of(j * size, size), size)] = (acc.T * scale).astype(BF16)

    def key_grads(t, j):
        pltpu.make_async_copy(aux.at[t, j], aux.at[t, j], aux_recv.at[t - 1, j]).wait()
        log_norm = jnp.concatenate([aux[t, j, r : r + 1, :] for r in range(4)], axis=1)
        offset = jnp.concatenate([aux[t, j, r + 4 : r + 5, :] for r in range(4)], axis=1)
        query, grad = blk[t, QUERY, j], blk[t, GRAD, j]
        for part in range(4):
            at = pl.ds(part * 128, 128)
            scores = nt(blk[WINDOW, KEY, j, at, :], query) * scale2
            w = jnp.exp2(scores - log_norm)
            dweights = nt(blk[WINDOW, VALUE, j, at, :], grad)
            ds = (w * (dweights - offset)).astype(BF16)
            key_acc[at, :] += nn(ds, query)
            value_acc[at, :] += nn(w.astype(BF16), grad)

    def clear_accs():
        key_acc[...] = jnp.zeros_like(key_acc)
        value_acc[...] = jnp.zeros_like(value_acc)

    def write_key_grads(j):
        lanes = pl.ds(pl.multiple_of(j * size, size), size)
        key_out[:, lanes] = key_acc[...] * scale
        value_out[:, lanes] = value_acc[...]

    def unit(u, do):
        @pl.when((u >= 0) & (u < UNITS))
        def _():
            do(lax.rem(u, 8) // 2, 2 * (u // 8) + lax.rem(u, 2))

    def from_u(start, do):
        def one(u, carry):
            unit(u, do)
            return carry

        lax.fori_loop(0, start, one, 0)

    def home(j, b):
        part = blk.at[0, b, j, 0 : block - rows, :]
        pltpu.make_async_copy(part, part, home_recv.at[j, b]).wait()
        to_next_chip(0, j, b)
        to_sibling(0, 1, 0, j, b)

    def near(j, b):
        await_slot(2, j, b)
        to_next_chip(2, j, b)
        to_sibling(2, 3, 0, j, b)
        to_sibling(2, 1, 1, j, b)

    def far(j, b):
        await_slot(4, j, b)
        to_sibling(4, 3, 1, j, b)

    from_u(HOP_LEAD, send_hops)
    from_u(LEAD, send_unit)
    from_u(BORDER_LEAD, send_border)
    pltpu.make_async_copy(blk.at[0, 0, 0:2], blk.at[0, 0, 0:2], own_sem).wait()

    def ticks(tick, carry):
        unit(tick, home)
        unit(tick - 1, near)
        unit(tick - 2, far)
        unit(tick + HOP_LEAD, send_hops)
        unit(tick + LEAD, send_unit)
        unit(tick + BORDER_LEAD, send_border)
        unit(tick - 2, functools.partial(await_slot, 1))
        unit(tick - 3, functools.partial(await_slot, 3))

        def at_turn(by, do):
            j = (tick - by) // 2

            @pl.when((lax.rem(tick + 64 - by, 2) == 0) & (j >= 0) & (j < heads))
            def _():
                do(j)

        def first_keys(j):
            clear_accs()
            key_grads(2, j)

        def more_keys(j):
            query_grads(j)
            key_grads(1, j)
            key_grads(4, j)

        def last_keys(j):
            key_grads(3, j)
            write_key_grads(j)

        at_turn(3, norms)
        at_turn(12, last_keys)
        at_turn(10, first_keys)
        at_turn(11, more_keys)
        return carry

    lax.fori_loop(0, UNITS + 3, ticks, 0)

    part = blk.at[0, :, :, 0 : block - rows, :]
    pltpu.make_async_copy(part, part, home_send).wait()
    part = aux.at[1 : WINDOW + 1]
    pltpu.make_async_copy(part, part, aux_send).wait()

    part = blk.at[0:2]
    pltpu.make_async_copy(part, part, ring_send).wait()

    @pl.when(i < 6)
    def _():
        pltpu.make_async_copy(part, part, ring_send).wait()

    @pl.when(sends_border)
    def _():
        pltpu.make_async_copy(blk.at[0], blk.at[0], border_send).wait()

    @pl.when(sends_hop)
    def _():
        pltpu.make_async_copy(blk.at[0], blk.at[0], hop_send).wait()


def body(query_states, key_states, value_states, output_grad, saved_offset, rest_mass):
    rest, offset = rest_mass.transpose(0, 2, 1), saved_offset.transpose(0, 2, 1)
    any_spec = pl.BlockSpec(memory_space=pl.ANY)
    vmem = pl.BlockSpec(memory_space=pltpu.VMEM)
    dma = pltpu.SemaphoreType.DMA
    outs = pl.pallas_call(
        kernel,
        out_shape=(
            pltpu.VMEM((512, 512), BF16),
            pltpu.VMEM((512, 512), F32),
            pltpu.VMEM((512, 512), F32),
        ),
        in_specs=[any_spec] * 4 + [vmem] * 2,
        out_specs=(vmem,) * 3,
        scratch_shapes=[
            pltpu.VMEM((4, 64, 4096), BF16),
            pltpu.VMEM((WINDOW + 1, 4, 4, 512, 128), BF16),
            pltpu.VMEM((4, 4, 8, 64, 128), BF16),
            pltpu.VMEM((WINDOW + 1, 4, 8, 128), F32),
            pltpu.VMEM((4, WINDOW, 512, 512), F32),
            pltpu.VMEM((512, 512), BF16),
            pltpu.VMEM((512, 128), F32),
            pltpu.VMEM((512, 128), F32),
            pltpu.VMEM((4, 1, 512), F32),
            pltpu.VMEM((4, 1, 512), F32),
            dma,
            dma((4, 4)),
            dma,
            dma((4,)),
            dma,
            dma((WINDOW, 4, 4)),
            dma,
            dma((4, 4)),
            dma,
            dma,
            dma((WINDOW, 4)),
        ],
        compiler_params=pltpu.CompilerParams(
            collective_id=0, has_side_effects=True, vmem_limit_bytes=60 << 20
        ),
        cost_estimate=pl.CostEstimate(
            flops=7_500_000_000, bytes_accessed=5_000_000, transcendentals=8_400_000
        ),
    )(key_states, query_states, value_states, output_grad, rest, offset)
    return tuple(out.reshape(8, 64, 512) for out in outs)


def solution(mesh):
    tokens = P("head", ("outer", "inner"), None)
    heads = P(None, ("outer", "inner"), "head")
    return jax.shard_map(
        body,
        mesh=mesh,
        in_specs=(tokens, tokens, tokens, tokens, heads, heads),
        out_specs=(heads, heads, heads),
        check_vma=False,
    )
```

```python
import functools
import math

import jax
import jax.numpy as jnp
from jax import lax
from jax.experimental import pallas as pl
from jax.experimental.pallas import tpu as pltpu
from jax.sharding import PartitionSpec as P

MESH = pl.DeviceIdType.MESH
F32 = jnp.float32
BF16 = jnp.bfloat16

KEY, QUERY, VALUE, GRAD = range(4)
UNITS = 16
WINDOW = 4
PEER_ORDER = (4, 3, 5, 2, 6, 1, 7)
BORDER_SENDERS = {0: (0, 4), 1: (7, 3)}
LEADS = ((5, 4), (9, 3), (UNITS, 2))
BORDER_MORE = 1
HOP_MORE = BORDER_MORE + 2


def nt(a, b):
    return lax.dot_general(a, b, (((1,), (1,)), ((), ())), preferred_element_type=F32)


def nn(a, b):
    return lax.dot_general(a, b, (((1,), (0,)), ((), ())), preferred_element_type=F32)


def tn(a, b):
    return lax.dot_general(a, b, (((0,), (0,)), ((), ())), preferred_element_type=F32)


def kernel(
    keys, queries, values, grads, rest_in, offset_in, query_out, key_out, value_out,
    staged, blk, hop, aux, weights, dscores, key_acc, value_acc, row_factor, offsets,
    home_send, home_recv, own_sem, stage_sem, ring_send, ring_recv, hop_send, hop_recv,
    border_send, aux_send, aux_recv,
):
    h, o, i = lax.axis_index("head"), lax.axis_index("outer"), lax.axis_index("inner")
    inputs = (keys, queries, values, grads)
    heads = 4
    rows, size = 64, 128
    block = 8 * rows
    scale = float(size) ** -0.5
    scale2 = scale * math.log2(math.e)
    core = lax.rem(i, 2)
    sibling = i + 1 - 2 * core
    next_o, last_o = lax.rem(o + 1, 8), lax.rem(o + 7, 8)
    my_rows = pl.ds(pl.multiple_of(h * rows, rows), rows)

    def ahead(by):
        at = i + by
        return (h, jnp.where(at > 7, next_o, o), lax.rem(at, 8))

    def behind(by):
        at = i + 8 - by
        return (h, jnp.where(at < 8, last_o, o), lax.rem(at, 8))

    barrier = pltpu.get_barrier_semaphore()

    def greet(device):
        pl.semaphore_signal(barrier, inc=1, device_id=device, device_id_type=MESH)

    for receiver, senders in BORDER_SENDERS.items():

        @pl.when(i == receiver)
        def _():
            for d in range(8):
                for sender in senders:
                    greet((lax.rem(h + d, 8), last_o, sender))

    for d in range(1, 8):
        greet((lax.rem(h + d, 8), o, i))
    for d in range(1, WINDOW + 1):
        greet(behind(d))

    @pl.when(core == 0)
    def _():
        greet((h, o, sibling))

    @pl.when(i == 3)
    def _():
        greet((h, o, 5))

    @pl.when(i == 0)
    def _():
        greet((h, o, 6))

    sends_border = (i == 0) | (i == 3) | (i == 4) | (i == 7)
    sends_hop = (i == 5) | (i == 6)
    relays = (i == 0) | (i == 3)

    def stage(a):
        return pltpu.make_async_copy(inputs[a].at[0], staged.at[a], stage_sem.at[a])

    for a in range(4):
        stage(a).start()

    pl.semaphore_wait(
        barrier, 7 + WINDOW + core + jnp.where(sends_border, 8, 0) + jnp.where(sends_hop, 1, 0)
    )

    for a in range(4):
        stage(a).wait()

    for a in range(4):
        for j in range(heads):
            pltpu.make_async_copy(
                staged.at[a, :, pl.ds(pl.multiple_of(h * 512 + j * size, size), size)],
                blk.at[0, a, j, my_rows, :],
                own_sem,
            ).start()

    def columns(t, j):
        return pl.ds(pl.multiple_of(t * 512 + j * size, size), size)

    def hop_copy(j, a, t):
        return pltpu.make_async_remote_copy(
            src_ref=staged.at[a, :, columns(t, j)],
            dst_ref=hop.at[a, j, t],
            send_sem=hop_send,
            recv_sem=hop_recv.at[j, a],
            device_id=(h, o, jnp.where(i == 5, 3, 0)),
            device_id_type=MESH,
        )

    def border_copy(j, a, t, slot, source):
        return pltpu.make_async_remote_copy(
            src_ref=source,
            dst_ref=blk.at[slot, a, j, my_rows, :],
            send_sem=border_send,
            recv_sem=ring_recv.at[slot - 1, j, a],
            device_id=(t, next_o, jnp.where((i == 3) | (i == 7), 1, 0)),
            device_id_type=MESH,
        )

    def send_hops(j, a):
        @pl.when(sends_hop)
        def _():
            for t in range(8):
                hop_copy(j, a, t).start()

    def send_unit(j, a):
        for d in PEER_ORDER:
            t = lax.rem(h + d, 8)
            pltpu.make_async_remote_copy(
                src_ref=staged.at[a, :, columns(t, j)],
                dst_ref=blk.at[0, a, j, my_rows, :],
                send_sem=home_send,
                recv_sem=home_recv.at[j, a],
                device_id=(t, o, i),
                device_id_type=MESH,
            ).start()

    def send_border(j, a):
        @pl.when((i == 4) | (i == 7))
        def _():
            slot = jnp.where(i == 4, 4, 2)
            for d in range(8):
                t = lax.rem(h + d, 8)
                border_copy(j, a, t, slot, staged.at[a, :, columns(t, j)]).start()

        @pl.when(relays)
        def _():
            slot = jnp.where(i == 0, 2, 4)
            pltpu.make_async_copy(hop.at[a, j], hop.at[a, j], hop_recv.at[j, a]).wait()
            for d in range(8):
                t = lax.rem(h + d, 8)
                border_copy(j, a, t, slot, hop.at[a, j, t]).start()

    def pass_on(slot, to_slot, to, j, a):
        pltpu.make_async_remote_copy(
            src_ref=blk.at[slot, a, j],
            dst_ref=blk.at[to_slot, a, j],
            send_sem=ring_send,
            recv_sem=ring_recv.at[to_slot - 1, j, a],
            device_id=(h, o, to),
            device_id_type=MESH,
        ).start()

    def to_next_chip(slot, j, a):
        @pl.when(i < 6)
        def _():
            pass_on(slot, slot + 2, lax.rem(i + 2, 8), j, a)

    def to_sibling(slot, to_slot, from_core, j, a):
        @pl.when(core == from_core)
        def _():
            pass_on(slot, to_slot, sibling, j, a)

    def await_slot(s, j, a):
        part = blk.at[s, a, j]
        pltpu.make_async_copy(part, part, ring_recv.at[s - 1, j, a]).wait()

    def aux_copy(j, by):
        return pltpu.make_async_remote_copy(
            src_ref=aux.at[0, j],
            dst_ref=aux.at[by, j],
            send_sem=aux_send,
            recv_sem=aux_recv.at[by - 1, j],
            device_id=ahead(by),
            device_id_type=MESH,
        )

    def row_of(ref, j):
        return jnp.concatenate([ref[a, pl.ds(j, 1), :] for a in range(8)], axis=1)

    def norms(j):
        query = blk[0, QUERY, j]
        row_max = jnp.full((1, block), -jnp.inf, F32)
        for s in range(WINDOW):
            scores = nt(blk[s, KEY, j], query) * scale2
            weights[j, s] = scores
            row_max = jnp.maximum(row_max, jnp.max(scores, axis=0, keepdims=True))
        row_sum = jnp.zeros((1, block), F32)
        for s in range(WINDOW):
            e = jnp.exp2(weights[j, s] - row_max)
            weights[j, s] = e
            row_sum = row_sum + jnp.sum(e, axis=0, keepdims=True)
        rest = row_of(rest_in, j) * math.log2(math.e)
        offset = row_of(offset_in, j)
        offsets[j] = offset
        ceiling = jnp.maximum(row_max, rest)
        total = row_sum * jnp.exp2(row_max - ceiling) + jnp.exp2(rest - ceiling)
        log_norm = ceiling + jnp.log2(total)
        row_factor[j] = jnp.exp2(row_max - log_norm)
        for r in range(4):
            lanes = slice(r * 128, (r + 1) * 128)
            aux[0, j, r : r + 1, :] = log_norm[:, lanes]
            aux[0, j, r + 4 : r + 5, :] = offset[:, lanes]
        for by in range(1, WINDOW + 1):
            aux_copy(j, by).start()

    def query_grads(j):
        grad = blk[0, GRAD, j]
        offset = offsets[j]
        factor = row_factor[j]
        acc = jnp.zeros((size, block), F32)
        for s in range(WINDOW):
            dweights = nt(blk[s, VALUE, j], grad)
            dscores[...] = ((weights[j, s] * factor) * (dweights - offset)).astype(BF16)
            acc = acc + tn(blk[s, KEY, j], dscores[...])
        query_out[:, pl.ds(pl.multiple_of(j * size, size), size)] = (acc.T * scale).astype(BF16)

    def key_grads(t, j):
        pltpu.make_async_copy(aux.at[t, j], aux.at[t, j], aux_recv.at[t - 1, j]).wait()
        log_norm = jnp.concatenate([aux[t, j, r : r + 1, :] for r in range(4)], axis=1)
        offset = jnp.concatenate([aux[t, j, r + 4 : r + 5, :] for r in range(4)], axis=1)
        query, grad = blk[t, QUERY, j], blk[t, GRAD, j]
        scores = nt(blk[WINDOW, KEY, j], query) * scale2
        w = jnp.exp2(scores - log_norm)
        dweights = nt(blk[WINDOW, VALUE, j], grad)
        ds = (w * (dweights - offset)).astype(BF16)
        key_acc[...] += nn(ds, query)
        value_acc[...] += nn(w.astype(BF16), grad)

    def clear_accs():
        key_acc[...] = jnp.zeros_like(key_acc)
        value_acc[...] = jnp.zeros_like(value_acc)

    def write_key_grads(j):
        lanes = pl.ds(pl.multiple_of(j * size, size), size)
        key_out[:, lanes] = key_acc[...] * scale
        value_out[:, lanes] = value_acc[...]

    def unit(u, do):
        @pl.when((u >= 0) & (u < UNITS))
        def _():
            do(lax.rem(u, 8) // 2, 2 * (u // 8) + lax.rem(u, 2))

    def from_u(start, do):
        def one(u, carry):
            unit(u, do)
            return carry

        lax.fori_loop(0, start, one, 0)

    def home(j, b):
        part = blk.at[0, b, j, 0 : block - rows, :]
        pltpu.make_async_copy(part, part, home_recv.at[j, b]).wait()
        to_next_chip(0, j, b)
        to_sibling(0, 1, 0, j, b)

    def near(j, b):
        await_slot(2, j, b)
        to_next_chip(2, j, b)
        to_sibling(2, 3, 0, j, b)
        to_sibling(2, 1, 1, j, b)

    def far(j, b):
        await_slot(4, j, b)
        to_sibling(4, 3, 1, j, b)

    from_u(LEADS[0][1] + HOP_MORE, send_hops)
    from_u(LEADS[0][1], send_unit)
    from_u(LEADS[0][1] + BORDER_MORE, send_border)
    pltpu.make_async_copy(blk.at[0, 0, 0:2], blk.at[0, 0, 0:2], own_sem).wait()

    def ticks(tick, carry):
        unit(tick, home)
        unit(tick - 1, near)
        unit(tick - 2, far)
        first = 0
        for last, lead in LEADS:

            @pl.when((tick >= first) & (tick <= last))
            def _():
                unit(tick + lead + HOP_MORE, send_hops)
                unit(tick + lead, send_unit)
                unit(tick + lead + BORDER_MORE, send_border)

            first = last + 2
        unit(tick - 2, functools.partial(await_slot, 1))
        unit(tick - 3, functools.partial(await_slot, 3))

        def at_turn(by, do):
            j = (tick - by) // 2

            @pl.when((lax.rem(tick + 64 - by, 2) == 0) & (j >= 0) & (j < heads))
            def _():
                do(j)

        def first_keys(j):
            clear_accs()
            key_grads(2, j)

        def more_keys(j):
            query_grads(j)
            key_grads(1, j)
            key_grads(4, j)

        def last_keys(j):
            key_grads(3, j)
            write_key_grads(j)

        at_turn(3, norms)
        at_turn(12, last_keys)
        at_turn(10, first_keys)
        at_turn(11, more_keys)
        return carry

    lax.fori_loop(0, UNITS + 3, ticks, 0)

    part = blk.at[0, :, :, 0 : block - rows, :]
    pltpu.make_async_copy(part, part, home_send).wait()
    part = aux.at[1 : WINDOW + 1]
    pltpu.make_async_copy(part, part, aux_send).wait()

    part = blk.at[0:2]
    pltpu.make_async_copy(part, part, ring_send).wait()

    @pl.when(i < 6)
    def _():
        pltpu.make_async_copy(part, part, ring_send).wait()

    @pl.when(sends_border)
    def _():
        pltpu.make_async_copy(blk.at[0], blk.at[0], border_send).wait()

    @pl.when(sends_hop)
    def _():
        pltpu.make_async_copy(blk.at[0], blk.at[0], hop_send).wait()


def body(query_states, key_states, value_states, output_grad, saved_offset, rest_mass):
    rest, offset = rest_mass.transpose(0, 2, 1), saved_offset.transpose(0, 2, 1)
    any_spec = pl.BlockSpec(memory_space=pl.ANY)
    vmem = pl.BlockSpec(memory_space=pltpu.VMEM)
    dma = pltpu.SemaphoreType.DMA
    outs = pl.pallas_call(
        kernel,
        out_shape=(
            pltpu.VMEM((512, 512), BF16),
            pltpu.VMEM((512, 512), F32),
            pltpu.VMEM((512, 512), F32),
        ),
        in_specs=[any_spec] * 4 + [vmem] * 2,
        out_specs=(vmem,) * 3,
        scratch_shapes=[
            pltpu.VMEM((4, 64, 4096), BF16),
            pltpu.VMEM((WINDOW + 1, 4, 4, 512, 128), BF16),
            pltpu.VMEM((4, 4, 8, 64, 128), BF16),
            pltpu.VMEM((WINDOW + 1, 4, 8, 128), F32),
            pltpu.VMEM((4, WINDOW, 512, 512), F32),
            pltpu.VMEM((512, 512), BF16),
            pltpu.VMEM((512, 128), F32),
            pltpu.VMEM((512, 128), F32),
            pltpu.VMEM((4, 1, 512), F32),
            pltpu.VMEM((4, 1, 512), F32),
            dma,
            dma((4, 4)),
            dma,
            dma((4,)),
            dma,
            dma((WINDOW, 4, 4)),
            dma,
            dma((4, 4)),
            dma,
            dma,
            dma((WINDOW, 4)),
        ],
        compiler_params=pltpu.CompilerParams(
            collective_id=0, has_side_effects=True, vmem_limit_bytes=60 << 20
        ),
        cost_estimate=pl.CostEstimate(
            flops=7_500_000_000, bytes_accessed=5_000_000, transcendentals=8_400_000
        ),
    )(key_states, query_states, value_states, output_grad, rest, offset)
    return tuple(out.reshape(8, 64, 512) for out in outs)


def solution(mesh):
    tokens = P("head", ("outer", "inner"), None)
    heads = P(None, ("outer", "inner"), "head")
    return jax.shard_map(
        body,
        mesh=mesh,
        in_specs=(tokens, tokens, tokens, tokens, heads, heads),
        out_specs=(heads, heads, heads),
        check_vma=False,
    )
```

```python
import functools
import math

import jax
import jax.numpy as jnp
from jax import lax
from jax.experimental import pallas as pl
from jax.experimental.pallas import tpu as pltpu
from jax.sharding import PartitionSpec as P

MESH = pl.DeviceIdType.MESH
F32 = jnp.float32
BF16 = jnp.bfloat16

KEY, QUERY, VALUE, GRAD = range(4)
UNITS = 16
DIRECT_FROM = 14
WINDOW = 4
PEER_ORDER = (4, 3, 5, 2, 6, 1, 7)
BORDER_SENDERS = {0: (0, 4), 1: (7, 3)}
LEADS = ((5, 4), (9, 3), (UNITS, 2))
BORDER_MORE = 1
HOP_MORE = BORDER_MORE + 2


def nt(a, b):
    return lax.dot_general(a, b, (((1,), (1,)), ((), ())), preferred_element_type=F32)


def nn(a, b):
    return lax.dot_general(a, b, (((1,), (0,)), ((), ())), preferred_element_type=F32)


def tn(a, b):
    return lax.dot_general(a, b, (((0,), (0,)), ((), ())), preferred_element_type=F32)


def kernel(
    keys, queries, values, grads, rest_in, offset_in, query_out, key_out, value_out,
    staged, blk, hop, aux, weights, dscores, key_acc, value_acc, row_factor, offsets,
    home_send, home_recv, direct_send, own_sem, stage_sem, ring_send, ring_recv, hop_send, hop_recv,
    border_send, aux_send, aux_recv,
):
    h, o, i = lax.axis_index("head"), lax.axis_index("outer"), lax.axis_index("inner")
    inputs = (keys, queries, values, grads)
    heads = 4
    rows, size = 64, 128
    block = 8 * rows
    scale = float(size) ** -0.5
    scale2 = scale * math.log2(math.e)
    core = lax.rem(i, 2)
    sibling = i + 1 - 2 * core
    next_o, last_o = lax.rem(o + 1, 8), lax.rem(o + 7, 8)
    my_rows = pl.ds(pl.multiple_of(h * rows, rows), rows)

    def ahead(by):
        at = i + by
        return (h, jnp.where(at > 7, next_o, o), lax.rem(at, 8))

    def behind(by):
        at = i + 8 - by
        return (h, jnp.where(at < 8, last_o, o), lax.rem(at, 8))

    barrier = pltpu.get_barrier_semaphore()

    def greet(device):
        pl.semaphore_signal(barrier, inc=1, device_id=device, device_id_type=MESH)

    for receiver, senders in BORDER_SENDERS.items():

        @pl.when(i == receiver)
        def _():
            for d in range(8):
                for sender in senders:
                    greet((lax.rem(h + d, 8), last_o, sender))

    for d in range(1, 8):
        greet((lax.rem(h + d, 8), o, i))
    for d in range(1, WINDOW + 1):
        greet(behind(d))

    @pl.when(core == 0)
    def _():
        greet((h, o, sibling))

    @pl.when(i == 3)
    def _():
        greet((h, o, 5))

    @pl.when(i == 0)
    def _():
        greet((h, o, 6))

    sends_border = (i == 0) | (i == 3) | (i == 4) | (i == 7)
    sends_hop = (i == 5) | (i == 6)
    relays = (i == 0) | (i == 3)

    def stage(a):
        return pltpu.make_async_copy(inputs[a].at[0], staged.at[a], stage_sem.at[a])

    for a in range(4):
        stage(a).start()

    pl.semaphore_wait(
        barrier, 7 + WINDOW + core + jnp.where(sends_border, 8, 0) + jnp.where(sends_hop, 1, 0)
    )

    for a in range(4):
        stage(a).wait()

    for a in range(4):
        for j in range(heads):
            pltpu.make_async_copy(
                staged.at[a, :, pl.ds(pl.multiple_of(h * 512 + j * size, size), size)],
                blk.at[0, a, j, my_rows, :],
                own_sem,
            ).start()

    def columns(t, j):
        return pl.ds(pl.multiple_of(t * 512 + j * size, size), size)

    def hop_copy(j, a, t):
        return pltpu.make_async_remote_copy(
            src_ref=staged.at[a, :, columns(t, j)],
            dst_ref=hop.at[a, j, t],
            send_sem=hop_send,
            recv_sem=hop_recv.at[j, a],
            device_id=(h, o, jnp.where(i == 5, 3, 0)),
            device_id_type=MESH,
        )

    def border_copy(j, a, t, slot, source):
        return pltpu.make_async_remote_copy(
            src_ref=source,
            dst_ref=blk.at[slot, a, j, my_rows, :],
            send_sem=border_send,
            recv_sem=ring_recv.at[slot - 1, j, a],
            device_id=(t, next_o, jnp.where((i == 3) | (i == 7), 1, 0)),
            device_id_type=MESH,
        )

    def send_hops(j, a):
        @pl.when(sends_hop)
        def _():
            for t in range(8):
                hop_copy(j, a, t).start()

    def send_unit(j, a):
        for d in PEER_ORDER:
            t = lax.rem(h + d, 8)
            pltpu.make_async_remote_copy(
                src_ref=staged.at[a, :, columns(t, j)],
                dst_ref=blk.at[0, a, j, my_rows, :],
                send_sem=home_send,
                recv_sem=home_recv.at[j, a],
                device_id=(t, o, i),
                device_id_type=MESH,
            ).start()

    def send_border(j, a):
        @pl.when((i == 4) | (i == 7))
        def _():
            slot = jnp.where(i == 4, 4, 2)
            for d in range(8):
                t = lax.rem(h + d, 8)
                border_copy(j, a, t, slot, staged.at[a, :, columns(t, j)]).start()

        @pl.when(relays)
        def _():
            slot = jnp.where(i == 0, 2, 4)
            pltpu.make_async_copy(hop.at[a, j], hop.at[a, j], hop_recv.at[j, a]).wait()
            for d in range(8):
                t = lax.rem(h + d, 8)
                border_copy(j, a, t, slot, hop.at[a, j, t]).start()

    def pass_on(slot, to_slot, to, j, a, sent=ring_send):
        pltpu.make_async_remote_copy(
            src_ref=blk.at[slot, a, j],
            dst_ref=blk.at[to_slot, a, j],
            send_sem=sent,
            recv_sem=ring_recv.at[to_slot - 1, j, a],
            device_id=(h, o, to),
            device_id_type=MESH,
        ).start()

    def to_next_chip(slot, j, a):
        @pl.when(i < 6)
        def _():
            pass_on(slot, slot + 2, lax.rem(i + 2, 8), j, a)

    def to_sibling(slot, to_slot, from_core, j, a):
        @pl.when(core == from_core)
        def _():
            pass_on(slot, to_slot, sibling, j, a)

    def await_slot(s, j, a):
        part = blk.at[s, a, j]
        pltpu.make_async_copy(part, part, ring_recv.at[s - 1, j, a]).wait()

    def aux_copy(j, by):
        return pltpu.make_async_remote_copy(
            src_ref=aux.at[0, j],
            dst_ref=aux.at[by, j],
            send_sem=aux_send,
            recv_sem=aux_recv.at[by - 1, j],
            device_id=ahead(by),
            device_id_type=MESH,
        )

    def row_of(ref, j):
        return jnp.concatenate([ref[a, pl.ds(j, 1), :] for a in range(8)], axis=1)

    def norms(j):
        query = blk[0, QUERY, j]
        row_max = jnp.full((1, block), -jnp.inf, F32)
        for s in range(WINDOW):
            scores = nt(blk[s, KEY, j], query) * scale2
            weights[j, s] = scores
            row_max = jnp.maximum(row_max, jnp.max(scores, axis=0, keepdims=True))
        row_sum = jnp.zeros((1, block), F32)
        for s in range(WINDOW):
            e = jnp.exp2(weights[j, s] - row_max)
            weights[j, s] = e
            row_sum = row_sum + jnp.sum(e, axis=0, keepdims=True)
        rest = row_of(rest_in, j) * math.log2(math.e)
        offset = row_of(offset_in, j)
        offsets[j] = offset
        ceiling = jnp.maximum(row_max, rest)
        total = row_sum * jnp.exp2(row_max - ceiling) + jnp.exp2(rest - ceiling)
        log_norm = ceiling + jnp.log2(total)
        row_factor[j] = jnp.exp2(row_max - log_norm)
        for r in range(4):
            lanes = slice(r * 128, (r + 1) * 128)
            aux[0, j, r : r + 1, :] = log_norm[:, lanes]
            aux[0, j, r + 4 : r + 5, :] = offset[:, lanes]
        for by in range(1, WINDOW + 1):
            aux_copy(j, by).start()

    def query_grads(j):
        grad = blk[0, GRAD, j]
        offset = offsets[j]
        factor = row_factor[j]
        acc = jnp.zeros((size, block), F32)
        for s in range(WINDOW):
            dweights = nt(blk[s, VALUE, j], grad)
            dscores[...] = ((weights[j, s] * factor) * (dweights - offset)).astype(BF16)
            acc = acc + tn(blk[s, KEY, j], dscores[...])
        query_out[:, pl.ds(pl.multiple_of(j * size, size), size)] = (acc.T * scale).astype(BF16)

    def key_grads(t, j):
        pltpu.make_async_copy(aux.at[t, j], aux.at[t, j], aux_recv.at[t - 1, j]).wait()
        log_norm = jnp.concatenate([aux[t, j, r : r + 1, :] for r in range(4)], axis=1)
        offset = jnp.concatenate([aux[t, j, r + 4 : r + 5, :] for r in range(4)], axis=1)
        query, grad = blk[t, QUERY, j], blk[t, GRAD, j]
        scores = nt(blk[WINDOW, KEY, j], query) * scale2
        w = jnp.exp2(scores - log_norm)
        dweights = nt(blk[WINDOW, VALUE, j], grad)
        ds = (w * (dweights - offset)).astype(BF16)
        key_acc[...] += nn(ds, query)
        value_acc[...] += nn(w.astype(BF16), grad)

    def clear_accs():
        key_acc[...] = jnp.zeros_like(key_acc)
        value_acc[...] = jnp.zeros_like(value_acc)

    def write_key_grads(j):
        lanes = pl.ds(pl.multiple_of(j * size, size), size)
        key_out[:, lanes] = key_acc[...] * scale
        value_out[:, lanes] = value_acc[...]

    def unit(u, do):
        @pl.when((u >= 0) & (u < UNITS))
        def _():
            do(lax.rem(u, 8) // 2, 2 * (u // 8) + lax.rem(u, 2))

    def from_u(start, do):
        def one(u, carry):
            unit(u, do)
            return carry

        lax.fori_loop(0, start, one, 0)

    def is_late(j, b):
        return 8 * (b // 2) + 2 * j + lax.rem(b, 2) >= DIRECT_FROM

    def home(j, b):
        part = blk.at[0, b, j, 0 : block - rows, :]
        pltpu.make_async_copy(part, part, home_recv.at[j, b]).wait()
        to_next_chip(0, j, b)

        @pl.when(is_late(j, b) & (i < 4))
        def _():
            pass_on(0, 4, lax.rem(i + 4, 8), j, b, direct_send)

        to_sibling(0, 1, 0, j, b)

    def near(j, b):
        await_slot(2, j, b)

        @pl.when((i < 2) | jnp.logical_not(is_late(j, b)))
        def _():
            to_next_chip(2, j, b)

        to_sibling(2, 3, 0, j, b)
        to_sibling(2, 1, 1, j, b)

    def far(j, b):
        await_slot(4, j, b)
        to_sibling(4, 3, 1, j, b)

    from_u(LEADS[0][1] + HOP_MORE, send_hops)
    from_u(LEADS[0][1], send_unit)
    from_u(LEADS[0][1] + BORDER_MORE, send_border)
    pltpu.make_async_copy(blk.at[0, 0, 0:2], blk.at[0, 0, 0:2], own_sem).wait()

    def ticks(tick, carry):
        unit(tick, home)
        unit(tick - 1, near)
        unit(tick - 2, far)
        first = 0
        for last, lead in LEADS:

            @pl.when((tick >= first) & (tick <= last))
            def _():
                unit(tick + lead + HOP_MORE, send_hops)
                unit(tick + lead, send_unit)
                unit(tick + lead + BORDER_MORE, send_border)

            first = last + 2
        unit(tick - 2, functools.partial(await_slot, 1))
        unit(tick - 3, functools.partial(await_slot, 3))

        def at_turn(by, do):
            j = (tick - by) // 2

            @pl.when((lax.rem(tick + 64 - by, 2) == 0) & (j >= 0) & (j < heads))
            def _():
                do(j)

        def first_keys(j):
            clear_accs()
            key_grads(2, j)

        def more_keys(j):
            query_grads(j)
            key_grads(1, j)
            key_grads(4, j)

        def last_keys(j):
            key_grads(3, j)
            write_key_grads(j)

        at_turn(3, norms)
        at_turn(12, last_keys)
        at_turn(10, first_keys)
        at_turn(11, more_keys)
        return carry

    lax.fori_loop(0, UNITS + 3, ticks, 0)

    part = blk.at[0, :, :, 0 : block - rows, :]
    pltpu.make_async_copy(part, part, home_send).wait()
    part = aux.at[1 : WINDOW + 1]
    pltpu.make_async_copy(part, part, aux_send).wait()

    part = blk.at[0:2]
    pltpu.make_async_copy(part, part, ring_send).wait()

    whole = blk.at[0]

    @pl.when(i < 6)
    def _():
        pltpu.make_async_copy(whole, whole, ring_send).wait()

    @pl.when(i < 2)
    def _():
        pltpu.make_async_copy(whole, whole, ring_send).wait()

    late = UNITS - DIRECT_FROM

    @pl.when((i >= 2) & (i < 6))
    def _():
        for units in (8, DIRECT_FROM - 8):
            part = blk.at[0:units, 0, 0] if units <= WINDOW else blk.at[0 : units // 2, 0, 0:2]
            pltpu.make_async_copy(part, part, ring_send).wait()

    @pl.when(i < 4)
    def _():
        part = blk.at[0:late, 0, 0]
        pltpu.make_async_copy(part, part, direct_send).wait()

    @pl.when(sends_border)
    def _():
        pltpu.make_async_copy(blk.at[0], blk.at[0], border_send).wait()

    @pl.when(sends_hop)
    def _():
        pltpu.make_async_copy(blk.at[0], blk.at[0], hop_send).wait()


def body(query_states, key_states, value_states, output_grad, saved_offset, rest_mass):
    rest, offset = rest_mass.transpose(0, 2, 1), saved_offset.transpose(0, 2, 1)
    any_spec = pl.BlockSpec(memory_space=pl.ANY)
    vmem = pl.BlockSpec(memory_space=pltpu.VMEM)
    dma = pltpu.SemaphoreType.DMA
    outs = pl.pallas_call(
        kernel,
        out_shape=(
            pltpu.VMEM((512, 512), BF16),
            pltpu.VMEM((512, 512), F32),
            pltpu.VMEM((512, 512), F32),
        ),
        in_specs=[any_spec] * 4 + [vmem] * 2,
        out_specs=(vmem,) * 3,
        scratch_shapes=[
            pltpu.VMEM((4, 64, 4096), BF16),
            pltpu.VMEM((WINDOW + 1, 4, 4, 512, 128), BF16),
            pltpu.VMEM((4, 4, 8, 64, 128), BF16),
            pltpu.VMEM((WINDOW + 1, 4, 8, 128), F32),
            pltpu.VMEM((4, WINDOW, 512, 512), F32),
            pltpu.VMEM((512, 512), BF16),
            pltpu.VMEM((512, 128), F32),
            pltpu.VMEM((512, 128), F32),
            pltpu.VMEM((4, 1, 512), F32),
            pltpu.VMEM((4, 1, 512), F32),
            dma,
            dma((4, 4)),
            dma,
            dma,
            dma((4,)),
            dma,
            dma((WINDOW, 4, 4)),
            dma,
            dma((4, 4)),
            dma,
            dma,
            dma((WINDOW, 4)),
        ],
        compiler_params=pltpu.CompilerParams(
            collective_id=0, has_side_effects=True, vmem_limit_bytes=60 << 20
        ),
        cost_estimate=pl.CostEstimate(
            flops=7_500_000_000, bytes_accessed=5_000_000, transcendentals=8_400_000
        ),
    )(key_states, query_states, value_states, output_grad, rest, offset)
    return tuple(out.reshape(8, 64, 512) for out in outs)


def solution(mesh):
    tokens = P("head", ("outer", "inner"), None)
    heads = P(None, ("outer", "inner"), "head")
    return jax.shard_map(
        body,
        mesh=mesh,
        in_specs=(tokens, tokens, tokens, tokens, heads, heads),
        out_specs=(heads, heads, heads),
        check_vma=False,
    )
```
